512 devices in a mesh: users: 16 (over y_lo, x), items: 32 (over z, y_hi, core).
Axes of the slice: x: 4, y: 8 (y_hi: 2, y_lo: 4; y = y_hi * 4 + y_lo), z: 8, core: 2. Of those that a mesh axis runs over, the one named last changes fastest.
Arguments:
- histories: int32 [16, 256], replicated, may hold values from 0 to 1048575
- item_degree: int32 [1048576], P('items'), may hold values from 1 to 63
- user_degree: int32 [131072], P('users'), may hold values from 1 to 63
- tile_values: float32 [16, 32, 24, 128, 128], P('users', 'items'), may hold values from 0 to 1
- tile_rows: int32 [16, 32, 24], P('users', 'items'), may hold values from 0 to 63
- tile_cols: int32 [16, 32, 24], P('users', 'items'), may hold values from 0 to 255
- tile_count: int32 [16, 32], P('users', 'items'), may hold values from 1 to 24, as said below
Outputs:
- scores: float32 [16, 1048576], P('users', 'items')
The draws below stay inside these ranges and needn't reach their ends.
Inputs may be any that keep to these rules, and one draw needn't show every extreme that they name: `tile_count`: every device has 1 to 24 live slots, and some device has exactly 24.
All inputs are finite; a program needn't handle non-finite values.
Results may differ from the reference program's by a relative error of at most 0.0003.
Values sent between devices are 32-bit elements; how exact they have to be, the bound alone decides.
A program may use at most 64 MiB of HBM per device.

```python
import jax
import jax.numpy as jnp
from jax import lax

TILE = 128
ITEMS_DEV = 32768
USERS_DEV = 8192
TILES_DEV = 24
QUERIES = 16
HIST = 256
GRID_U = 16
GRID_I = 32
ITEMS = 1048576
USERS = 131072


def draw_tile_count(key, part):
    counts = jax.random.randint(key, (GRID_U * GRID_I,), 1, TILES_DEV + 1)
    chosen = jax.random.randint(jax.random.fold_in(key, 7), (), 0, GRID_U * GRID_I)
    positions = jnp.arange(GRID_U * GRID_I, dtype=jnp.int32)
    counts = jnp.where(positions == chosen, TILES_DEV, counts)
    return counts.reshape(GRID_U, GRID_I).astype(jnp.int32)


def with_ends(result, key, smallest, largest):
    longest = result.shape.index(max(result.shape))
    spots = []
    for shift in (0, 1):
        where = [jax.random.randint(jax.random.fold_in(key, axis), (), 0, length) for axis, length in enumerate(result.shape)]
        where[longest] = (where[longest] + shift) % result.shape[longest]
        spots.append(tuple(where))
    return result.at[spots[0]].set(smallest).at[spots[1]].set(largest)


def block_levels(key, dims, shards, least, largest):
    level, own = 1.0, jax.random.fold_in(key, 6)
    for axis_at, shards_of in shards:
        steps = jnp.exp(jax.random.uniform(jax.random.fold_in(own, axis_at), (shards_of,), jnp.float32, least / len(shards), largest / len(shards)))
        level = level * jnp.repeat(steps, dims[axis_at] // shards_of).reshape([-1 if axis == axis_at else 1 for axis in range(len(dims))])
    return level


def setup_inputs(seed: int = 0) -> dict:
    key_of = jax.random.split(jax.random.key(seed), 8)
    return {
        "histories": with_ends(jax.random.randint(key_of[0], (QUERIES, HIST), 0, ITEMS), jax.random.fold_in(key_of[0], 1), 0, ITEMS - 1).astype(jnp.int32),
        "item_degree": with_ends(jax.random.randint(key_of[1], (ITEMS,), 1, 64), jax.random.fold_in(key_of[1], 1), 1, 63).astype(jnp.int32),
        "user_degree": with_ends(jax.random.randint(key_of[2], (USERS,), 1, 64), jax.random.fold_in(key_of[2], 1), 1, 63).astype(jnp.int32),
        "tile_values": jnp.clip(1.0 * jax.random.uniform(key_of[3], (GRID_U, GRID_I, TILES_DEV, TILE, TILE), jnp.float32) ** block_levels(key_of[3], (GRID_U, GRID_I, TILES_DEV, TILE, TILE), ((0, 16), (1, 32)), -0.2, 0.2), 0.0, 1.0),
        "tile_rows": with_ends(jax.random.randint(key_of[4], (GRID_U, GRID_I, TILES_DEV), 0, USERS_DEV // TILE), jax.random.fold_in(key_of[4], 1), 0, (USERS_DEV // TILE) - 1).astype(jnp.int32),
        "tile_cols": with_ends(jax.random.randint(key_of[5], (GRID_U, GRID_I, TILES_DEV), 0, ITEMS_DEV // TILE), jax.random.fold_in(key_of[5], 1), 0, (ITEMS_DEV // TILE) - 1).astype(jnp.int32),
        "tile_count": draw_tile_count(jax.random.fold_in(key_of[7], 71), 0),
    }


def reference(histories, item_degree, user_degree, tile_values, tile_rows, tile_cols, tile_count):
    highest = lax.Precision.HIGHEST
    queries = histories.shape[0]
    user_blocks = USERS_DEV // TILE
    item_blocks = ITEMS_DEV // TILE
    query_ids = jnp.broadcast_to(jnp.arange(queries, dtype=jnp.int32)[:, None], histories.shape)
    hits = jnp.zeros((queries, ITEMS), jnp.float32).at[query_ids, histories].add(1.0)
    item_scale = lax.rsqrt(item_degree.astype(jnp.float32))
    query_panel = hits * item_scale[None, :]
    slot_ids = jnp.arange(TILES_DEV, dtype=jnp.int32)
    devices = jnp.arange(GRID_U * GRID_I, dtype=jnp.int32)

    def tile_parts(device):
        user_block = device // GRID_I
        item_block = device % GRID_I
        values_now = tile_values[user_block, item_block]
        alive_mask = (slot_ids < tile_count[user_block, item_block]).astype(jnp.float32)
        row_onehot = (tile_rows[user_block, item_block][:, None] == jnp.arange(user_blocks, dtype=jnp.int32)[None, :]).astype(jnp.float32) * alive_mask[:, None]
        col_onehot = (tile_cols[user_block, item_block][:, None] == jnp.arange(item_blocks, dtype=jnp.int32)[None, :]).astype(jnp.float32) * alive_mask[:, None]
        return (user_block, item_block, values_now, row_onehot, col_onehot)

    def first_pass(user_sums, device):
        user_block, item_block, values_now, row_onehot, col_onehot = tile_parts(device)
        panels = lax.dynamic_slice_in_dim(query_panel, item_block * ITEMS_DEV, ITEMS_DEV, 1).reshape(queries, item_blocks, TILE)
        picked = jnp.einsum('qbk,tb->qtk', panels, (col_onehot > 0).astype(jnp.float32), precision=highest)
        partial_value = jnp.einsum('qtk,tjk->qtj', picked, values_now, precision=highest)
        added = jnp.einsum('qtj,tu->quj', partial_value, row_onehot, precision=highest).reshape(queries, USERS_DEV)
        current = lax.dynamic_slice_in_dim(user_sums, user_block * USERS_DEV, USERS_DEV, 1)
        return (lax.dynamic_update_slice_in_dim(user_sums, current + added, user_block * USERS_DEV, 1), None)
    user_sums, _ = lax.scan(first_pass, jnp.zeros((queries, USERS), jnp.float32), devices)
    user_weights = user_sums / user_degree.astype(jnp.float32)[None, :]

    def second_pass(score_sums, device):
        user_block, item_block, values_now, row_onehot, col_onehot = tile_parts(device)
        blocks = lax.dynamic_slice_in_dim(user_weights, user_block * USERS_DEV, USERS_DEV, 1).reshape(queries, user_blocks, TILE)
        picked = jnp.einsum('quj,tu->qtj', blocks, (row_onehot > 0).astype(jnp.float32), precision=highest)
        partial_value = jnp.einsum('qtj,tjk->qtk', picked, values_now, precision=highest)
        added = jnp.einsum('qtk,tb->qbk', partial_value, col_onehot, precision=highest).reshape(queries, ITEMS_DEV)
        current = lax.dynamic_slice_in_dim(score_sums, item_block * ITEMS_DEV, ITEMS_DEV, 1)
        return (lax.dynamic_update_slice_in_dim(score_sums, current + added, item_block * ITEMS_DEV, 1), None)
    score_sums, _ = lax.scan(second_pass, jnp.zeros((queries, ITEMS), jnp.float32), devices)
    return score_sums * item_scale[None, :]
```

```python
import functools

import jax
import jax.numpy as jnp
from jax import lax
from jax.experimental import pallas as pl
from jax.experimental.pallas import tpu as pltpu
from jax.sharding import PartitionSpec as P

MESH = pl.DeviceIdType.MESH
F32 = jnp.float32
BF16 = jnp.bfloat16
I32 = jnp.int32
NT = (((1,), (1,)), ((), ()))
NN = (((1,), (0,)), ((), ()))


def halves(x):
    high = x.astype(BF16)
    return high, (x - high.astype(F32)).astype(BF16)


def dot(a, b, dims=NN):
    return lax.dot_general(a, b, dims, preferred_element_type=F32)


def kernel(
    slots, queries, user_blocks, item_blocks, width,
    hist, ideg, udeg, vals_any, rows, cols, count,
    out,
    vals, vhi, vlo, hits, msg1, recv1, xsend, xrecv, msg2, recv2, msg3, recv3,
    meta_r_out, meta_r, meta_c_out, meta_c, pick_r, pick_rt, pick_c, sem,
):
    n = queries
    span = slots * n
    items = lax.axis_index("items")
    user = lax.axis_index("users")
    chip, core = items // 2, lax.rem(items, 2)
    partner = {"items": chip * 2 + (1 - core)}

    def chip_peer(i):
        c = lax.rem(chip + 1 + i, n)
        return c, {"items": c * 2 + core}

    def user_peer(i):
        u = lax.rem(user + 1 + i, n)
        return u, {"users": u}

    def part(ref, i, size=slots):
        return ref.at[pl.ds(pl.multiple_of(i * size, 8), size)]

    def wait(ref, count_rows, k):
        piece = ref.at[pl.ds(0, count_rows)]
        pltpu.make_async_copy(piece, piece, sem.at[k]).wait()

    barrier = pltpu.get_barrier_semaphore()
    load = pltpu.make_async_copy(vals_any, vals, sem.at[0])
    load.start()

    @pl.loop(0, n - 1)
    def _(i):
        pl.semaphore_signal(barrier, inc=1, device_id=chip_peer(i)[1], device_id_type=MESH)
        pl.semaphore_signal(barrier, inc=1, device_id=user_peer(i)[1], device_id_type=MESH)

    pl.semaphore_signal(barrier, inc=1, device_id=partner, device_id_type=MESH)

    place = lax.broadcasted_iota(I32, (8, width), 0) * width + lax.broadcasted_iota(I32, (8, width), 1)
    sub = lax.broadcasted_iota(I32, (slots, width), 0)
    mrow = jnp.zeros((8, width), I32)
    mcol = jnp.zeros((8, width), I32)
    colv = jnp.zeros((slots, width), I32)
    alive = count[0, 0]
    for t in range(slots):
        r, c = rows[0, 0, t], cols[0, 0, t]
        live = t < alive
        mrow = jnp.where(place == chip * slots + t, jnp.where(live, r, -1), mrow)
        mcol = jnp.where(place == user * slots + t, jnp.where(live, c, -1), mcol)
        colv = jnp.where(sub == t, c, colv)
    meta_r_out[...] = mrow
    meta_c_out[...] = mcol
    part(meta_r, chip, 8)[...] = mrow
    part(meta_c, user, 8)[...] = mcol

    hlen = hist.shape[1]
    bits = width.bit_length() - 1
    colw = jnp.concatenate([colv] * (hlen // width), axis=1) + items * item_blocks
    lane_id = lax.broadcasted_iota(I32, (width, hlen), 0)
    for q in range(n):
        h = hist[q : q + 1, :]
        block = lax.shift_right_logical(h, bits) == colw
        spot = (h & (width - 1)) == lane_id
        hits[pl.ds(q, slots, stride=n), :] = dot(
            jnp.where(block, 1.0, 0.0).astype(BF16), jnp.where(spot, 1.0, 0.0).astype(BF16), NT
        )

    pl.semaphore_wait(barrier, 2 * (n - 1) + 1)

    @pl.loop(0, n - 1)
    def _(i):
        pltpu.make_async_remote_copy(
            meta_r_out, part(meta_r, chip, 8), sem.at[1], sem.at[2],
            device_id=chip_peer(i)[1], device_id_type=MESH,
        ).start()
        pltpu.make_async_remote_copy(
            meta_c_out, part(meta_c, user, 8), sem.at[3], sem.at[4],
            device_id=user_peer(i)[1], device_id_type=MESH,
        ).start()

    load.wait()

    for t in range(slots):
        degree = ideg[pl.ds(cols[0, 0, t], 1), :]
        high, low = halves(vals[t] * lax.rsqrt(degree.astype(F32)))
        vhi[t] = high
        vlo[t] = low
        h = hits[pl.ds(t * n, n), :].astype(BF16)
        msg1[pl.ds(t, n, stride=slots), :] = dot(h, high, NT) + dot(h, low, NT)

    def exchange(msg, recv, mine, peer, send_k, recv_k):
        @pl.loop(0, n - 1)
        def _(i):
            p, where = peer(i)
            pltpu.make_async_remote_copy(
                part(msg, p), part(recv, mine), sem.at[send_k], sem.at[recv_k],
                device_id=where, device_id_type=MESH,
            ).start()

        part(recv, mine)[...] = part(msg, mine)[...]

    exchange(msg1, recv1, chip, chip_peer, 5, 6)

    wait(meta_r, 8 * (n - 1), 2)
    wait(meta_c, 8 * (n - 1), 4)

    def gathered(ref):
        total = ref[0:8, :]
        for i in range(1, n):
            total = total + ref[8 * i : 8 * i + 8, :]
        return total

    ids_r, ids_c = gathered(meta_r), gathered(meta_c)
    block_r = lax.broadcasted_iota(I32, (width, width), 0)
    block_c = lax.broadcasted_iota(I32, (item_blocks, width), 0)
    for k in range(span // width):
        at = slice(k * width, (k + 1) * width)
        hot = jnp.where(ids_r[k : k + 1, :] == block_r, 1.0, 0.0)
        pick_r[:, at] = hot[:user_blocks].astype(BF16)
        pick_rt[at, :] = hot.T.astype(BF16)
        pick_c[:, at] = jnp.where(ids_c[k : k + 1, :] == block_c, 1.0, 0.0).astype(BF16)

    wait(recv1, slots * (n - 1), 6)
    high, low = halves(recv1[...])
    acc = dot(pick_r[...], high) + dot(pick_r[...], low)
    xsend[...] = acc
    cross = pltpu.make_async_remote_copy(
        xsend, xrecv, sem.at[7], sem.at[8], device_id=partner, device_id_type=MESH
    )
    cross.start()
    cross.wait()
    weights = (acc + xrecv[...]) / udeg[...].astype(F32)
    high, low = halves(weights)
    back = pick_rt[:, :user_blocks]
    msg2[...] = dot(back, high) + dot(back, low)
    exchange(msg2, recv2, chip, chip_peer, 9, 10)
    wait(recv2, slots * (n - 1), 10)

    for t in range(slots):
        high, low = halves(recv2[pl.ds(t, n, stride=slots), :])
        msg3[pl.ds(t, n, stride=slots), :] = dot(high, vhi[t]) + dot(low, vhi[t]) + dot(high, vlo[t])

    exchange(msg3, recv3, user, user_peer, 11, 12)
    wait(recv3, slots * (n - 1), 12)
    high, low = halves(recv3[...])
    out[...] = dot(pick_c[...], high) + dot(pick_c[...], low)

    wait(meta_r, 8 * (n - 1), 1)
    wait(meta_c, 8 * (n - 1), 3)
    wait(msg1, slots * (n - 1), 5)
    wait(msg2, slots * (n - 1), 9)
    wait(msg3, slots * (n - 1), 11)


def body(histories, item_degree, user_degree, tile_values, tile_rows, tile_cols, tile_count):
    queries = histories.shape[0]
    slots, width = tile_values.shape[2], tile_values.shape[-1]
    item_blocks = item_degree.shape[0] // width
    user_blocks = user_degree.shape[0] // width
    span = slots * queries
    vmem = pl.BlockSpec(memory_space=pltpu.VMEM)
    smem = pl.BlockSpec(memory_space=pltpu.SMEM)
    panel = pltpu.VMEM((span, width), F32)
    scores = pl.pallas_call(
        functools.partial(kernel, slots, queries, user_blocks, item_blocks, width),
        out_shape=jax.ShapeDtypeStruct((item_blocks, width), F32),
        in_specs=[vmem, vmem, vmem, pl.BlockSpec(memory_space=pl.ANY), smem, smem, smem],
        out_specs=vmem,
        scratch_shapes=[
            pltpu.VMEM((slots, width, width), F32),
            pltpu.VMEM((slots, width, width), BF16),
            pltpu.VMEM((slots, width, width), BF16),
            panel, panel, panel,
            pltpu.VMEM((user_blocks, width), F32),
            pltpu.VMEM((user_blocks, width), F32),
            panel, panel, panel, panel,
            pltpu.VMEM((8, width), I32),
            pltpu.VMEM((8 * queries, width), I32),
            pltpu.VMEM((8, width), I32),
            pltpu.VMEM((8 * queries, width), I32),
            pltpu.VMEM((user_blocks, span), BF16),
            pltpu.VMEM((span, width), BF16),
            pltpu.VMEM((item_blocks, span), BF16),
            pltpu.SemaphoreType.DMA((13,)),
        ],
        compiler_params=pltpu.CompilerParams(
            collective_id=0, has_side_effects=True, vmem_limit_bytes=32 * 1024 * 1024
        ),
        cost_estimate=pl.CostEstimate(flops=10**8, bytes_accessed=4 * 10**6, transcendentals=0),
    )(
        histories,
        item_degree.reshape(item_blocks, width),
        user_degree.reshape(user_blocks, width),
        tile_values.reshape(slots, width, width),
        tile_rows, tile_cols, tile_count,
    )
    return scores.reshape(1, item_blocks * width)


def solution(mesh):
    in_specs = (
        P(),
        P("items"),
        P("users"),
        P("users", "items", None, None, None),
        P("users", "items", None),
        P("users", "items", None),
        P("users", "items"),
    )
    out_specs = P("users", "items")
    return jax.shard_map(body, mesh=mesh, in_specs=in_specs, out_specs=out_specs, check_vma=False)
```

```python
import functools

import jax
import jax.numpy as jnp
from jax import lax
from jax.experimental import pallas as pl
from jax.experimental.pallas import tpu as pltpu
from jax.sharding import PartitionSpec as P

MESH = pl.DeviceIdType.MESH
F32 = jnp.float32
BF16 = jnp.bfloat16
I32 = jnp.int32
NT = (((1,), (1,)), ((), ()))
NN = (((1,), (0,)), ((), ()))


def halves(x):
    high = x.astype(BF16)
    return high, (x - high.astype(F32)).astype(BF16)


def dot(a, b, dims=NN):
    return lax.dot_general(a, b, dims, preferred_element_type=F32)


GROUPS = 4


def kernel(slots, queries, user_blocks, item_blocks, width, *refs):
    inputs, out, local = refs[:7], refs[7], refs[8:15]
    (
        vhi, vlo, hits, msg1, recv1, xsend, xrecv, msg2, recv2, msg3, recv3,
        meta_r_out, meta_r, meta_c_out, meta_c, pick_r, pick_rt, pick_c,
        load_sem, back_sem, sem,
    ) = refs[15:]
    hist, ideg, udeg, vals, rows, cols, count = local
    n = queries
    span = slots * n
    items = lax.axis_index("items")
    user = lax.axis_index("users")
    z, y_hi, core = items // 4, lax.rem(items // 2, 2), lax.rem(items, 2)
    run = n // 4
    chip = ((z // run) * 2 + y_hi) * run + lax.rem(z, run)
    partner = {"items": items + 1 - 2 * core}
    per = n // GROUPS

    def at_chip(c):
        z = (c // (2 * run)) * run + lax.rem(c, run)
        return {"items": (z * 2 + lax.rem(c // run, 2)) * 2 + core}

    def others(me, start, stop, action, backwards=False):
        @pl.loop(start, stop)
        def _(i):
            p = start + stop - 1 - i if backwards else i

            @pl.when(p != me)
            def _():
                action(p)

    def send(src, dst, send_k, recv_sem, where):
        pltpu.make_async_remote_copy(
            src, dst, sem.at[send_k], recv_sem, device_id=where, device_id_type=MESH
        ).start()

    def part(ref, i, size=slots):
        return ref.at[pl.ds(pl.multiple_of(i * size, 8), size)]

    def wait(ref, count_rows, k):
        piece = ref.at[pl.ds(0, count_rows)]
        pltpu.make_async_copy(piece, piece, sem.at[k]).wait()

    barrier = pltpu.get_barrier_semaphore()
    loads = [pltpu.make_async_copy(inputs[i], local[i], load_sem.at[i]) for i in range(7)]
    for i in (4, 5, 6, 0, 1, 3, 2):
        loads[i].start()

    def greet(where):
        pl.semaphore_signal(barrier, inc=1, device_id=where, device_id_type=MESH)

    others(chip, 0, n, lambda p: greet(at_chip(p)))
    others(user, 0, n, lambda p: greet({"users": p}))
    greet(partner)

    place = lax.broadcasted_iota(I32, (8, width), 0) * width + lax.broadcasted_iota(I32, (8, width), 1)
    sub = lax.broadcasted_iota(I32, (slots, width), 0)
    for i in (4, 5, 6):
        loads[i].wait()
    mrow = jnp.zeros((8, width), I32)
    mcol = jnp.zeros((8, width), I32)
    colv = jnp.zeros((slots, width), I32)
    alive = count[0, 0]
    for t in range(slots):
        r, c = rows[0, 0, t], cols[0, 0, t]
        live = t < alive
        mrow = jnp.where(place == chip * slots + t, jnp.where(live, r, -1), mrow)
        mcol = jnp.where(place == user * slots + t, jnp.where(live, c, -1), mcol)
        colv = jnp.where(sub == t, c, colv)
    meta_r_out[...] = mrow
    meta_c_out[...] = mcol
    part(meta_r, chip, 8)[...] = mrow
    part(meta_c, user, 8)[...] = mcol

    loads[0].wait()
    hlen = hist.shape[1]
    bits = width.bit_length() - 1
    colw = jnp.concatenate([colv] * (hlen // width), axis=1) + items * item_blocks
    lane_id = lax.broadcasted_iota(I32, (width, hlen), 0)
    for q in range(n):
        h = hist[q : q + 1, :]
        block = lax.shift_right_logical(h, bits) == colw
        spot = (h & (width - 1)) == lane_id
        hits[pl.ds(q, slots, stride=n), :] = dot(
            jnp.where(block, 1.0, 0.0).astype(BF16), jnp.where(spot, 1.0, 0.0).astype(BF16), NT
        )

    loads[1].wait()
    loads[3].wait()

    for t in range(slots):
        degree = ideg[pl.ds(cols[0, 0, t], 1), :]
        high, low = halves(vals[t] * lax.rsqrt(degree.astype(F32)))
        vhi[t] = high
        vlo[t] = low
        h = hits[pl.ds(t * n, n), :].astype(BF16)
        msg1[pl.ds(t, n, stride=slots), :] = dot(h, high, NT) + dot(h, low, NT)

    pl.semaphore_wait(barrier, 2 * (n - 1) + 1)

    def forth(p):
        send(meta_r_out, part(meta_r, chip, 8), 1, sem.at[2], at_chip(p))
        send(part(msg1, p), part(recv1, chip), 5, sem.at[6], at_chip(p))

    others(chip, 0, n, forth, backwards=True)
    part(recv1, chip)[...] = part(msg1, chip)[...]
    others(user, 0, n, lambda p: send(meta_c_out, part(meta_c, user, 8), 3, sem.at[4], {"users": p}))

    def gathered(ref):
        total = ref[0:8, :]
        for i in range(1, n):
            total = total + ref[8 * i : 8 * i + 8, :]
        return total

    wait(meta_r, 8 * (n - 1), 2)
    ids = gathered(meta_r)
    block = lax.broadcasted_iota(I32, (width, width), 0)
    for k in range(span // width):
        at = slice(k * width, (k + 1) * width)
        hot = jnp.where(ids[k : k + 1, :] == block, 1.0, 0.0)
        pick_r[:, at] = hot[:user_blocks].astype(BF16)
        pick_rt[at, :] = hot.T.astype(BF16)

    wait(recv1, slots * (n - 1), 6)
    high, low = halves(recv1[...])
    acc = dot(pick_r[...], high) + dot(pick_r[...], low)
    xsend[...] = acc
    cross = pltpu.make_async_remote_copy(
        xsend, xrecv, sem.at[7], sem.at[8], device_id=partner, device_id_type=MESH
    )
    cross.start()
    cross.wait()
    loads[2].wait()
    weights = (acc + xrecv[...]) / udeg[...].astype(F32)
    high, low = halves(weights)
    back = pick_rt[:, :user_blocks]
    msg2[...] = dot(back, high) + dot(back, low)
    mine = back_sem.at[chip // per]
    others(chip, 0, n, lambda p: send(part(msg2, p), part(recv2, chip), 9, mine, at_chip(p)))
    part(recv2, chip)[...] = part(msg2, chip)[...]

    wait(meta_c, 8 * (n - 1), 4)
    ids = gathered(meta_c)
    block = lax.broadcasted_iota(I32, (item_blocks, width), 0)
    for k in range(span // width):
        at = slice(k * width, (k + 1) * width)
        pick_c[:, at] = jnp.where(ids[k : k + 1, :] == block, 1.0, 0.0).astype(BF16)

    @pl.loop(0, GROUPS)
    def _(g):
        own = chip // per == g
        for came, senders in ((own, per - 1), (jnp.logical_not(own), per)):

            @pl.when(came)
            def _():
                piece = recv2.at[pl.ds(0, slots * senders)]
                pltpu.make_async_copy(piece, piece, back_sem.at[g]).wait()

        for t in range(slots):
            spots = pl.ds(g * (per * slots) + t, per, stride=slots)
            high, low = halves(recv2[spots, :])
            msg3[spots, :] = dot(high, vhi[t]) + dot(low, vhi[t]) + dot(high, vlo[t])

        others(
            user, g * per, (g + 1) * per,
            lambda p: send(part(msg3, p), part(recv3, user), 11, sem.at[12], {"users": p}),
        )

    part(recv3, user)[...] = part(msg3, user)[...]
    wait(recv3, slots * (n - 1), 12)
    high, low = halves(recv3[...])
    out[...] = dot(pick_c[...], high) + dot(pick_c[...], low)

    wait(meta_r, 8 * (n - 1), 1)
    wait(meta_c, 8 * (n - 1), 3)
    wait(msg1, slots * (n - 1), 5)
    wait(msg2, slots * (n - 1), 9)
    wait(msg3, slots * (n - 1), 11)


def body(histories, item_degree, user_degree, tile_values, tile_rows, tile_cols, tile_count):
    queries = histories.shape[0]
    slots, width = tile_values.shape[2], tile_values.shape[-1]
    item_blocks = item_degree.shape[0] // width
    user_blocks = user_degree.shape[0] // width
    span = slots * queries
    vmem = pl.BlockSpec(memory_space=pltpu.VMEM)
    panel = pltpu.VMEM((span, width), F32)
    scores = pl.pallas_call(
        functools.partial(kernel, slots, queries, user_blocks, item_blocks, width),
        out_shape=jax.ShapeDtypeStruct((item_blocks, width), F32),
        in_specs=[pl.BlockSpec(memory_space=pltpu.HBM)] * 7,
        out_specs=vmem,
        scratch_shapes=[
            pltpu.VMEM(histories.shape, I32),
            pltpu.VMEM((item_blocks, width), I32),
            pltpu.VMEM((user_blocks, width), I32),
            pltpu.VMEM((slots, width, width), F32),
            pltpu.SMEM(tile_rows.shape, I32),
            pltpu.SMEM(tile_cols.shape, I32),
            pltpu.SMEM(tile_count.shape, I32),
            pltpu.VMEM((slots, width, width), BF16),
            pltpu.VMEM((slots, width, width), BF16),
            panel, panel, panel,
            pltpu.VMEM((user_blocks, width), F32),
            pltpu.VMEM((user_blocks, width), F32),
            panel, panel, panel, panel,
            pltpu.VMEM((8, width), I32),
            pltpu.VMEM((8 * queries, width), I32),
            pltpu.VMEM((8, width), I32),
            pltpu.VMEM((8 * queries, width), I32),
            pltpu.VMEM((user_blocks, span), BF16),
            pltpu.VMEM((span, width), BF16),
            pltpu.VMEM((item_blocks, span), BF16),
            pltpu.SemaphoreType.DMA((7,)),
            pltpu.SemaphoreType.DMA((GROUPS,)),
            pltpu.SemaphoreType.DMA((13,)),
        ],
        compiler_params=pltpu.CompilerParams(
            collective_id=0, has_side_effects=True, vmem_limit_bytes=63 * 1024 * 1024
        ),
        cost_estimate=pl.CostEstimate(flops=10**8, bytes_accessed=4 * 10**6, transcendentals=0),
    )(
        histories,
        item_degree.reshape(item_blocks, width),
        user_degree.reshape(user_blocks, width),
        tile_values.reshape(slots, width, width),
        tile_rows, tile_cols, tile_count,
    )
    return scores.reshape(1, item_blocks * width)


def solution(mesh):
    in_specs = (
        P(),
        P("items"),
        P("users"),
        P("users", "items", None, None, None),
        P("users", "items", None),
        P("users", "items", None),
        P("users", "items"),
    )
    out_specs = P("users", "items")
    return jax.shard_map(body, mesh=mesh, in_specs=in_specs, out_specs=out_specs, check_vma=False)
```

```python
import functools

import jax
import jax.numpy as jnp
from jax import lax
from jax.experimental import pallas as pl
from jax.experimental.pallas import tpu as pltpu
from jax.sharding import PartitionSpec as P

MESH = pl.DeviceIdType.MESH
F32 = jnp.float32
BF16 = jnp.bfloat16
I32 = jnp.int32
NT = (((1,), (1,)), ((), ()))
NN = (((1,), (0,)), ((), ()))


def halves(x):
    high = x.astype(BF16)
    return high, (x - high.astype(F32)).astype(BF16)


def dot(a, b, dims=NN):
    return lax.dot_general(a, b, dims, preferred_element_type=F32)


GROUPS = 4


def kernel(slots, queries, user_blocks, item_blocks, width, *refs):
    inputs, out, local = refs[:7], refs[7], refs[8:15]
    (
        vhi, vlo, hits, msg1, recv1, xsend, xrecv, msg2, recv2, msg3, recv3,
        recv1b, xsendb, xrecvb, msg2b,
        meta_r_out, meta_r, meta_c_out, meta_c, pick_r, pick_rt, pick_c,
        load_sem, back_sem, ready, sem,
    ) = refs[15:]
    hist, ideg, udeg, vals, rows, cols, count = local
    n = queries
    span = slots * n
    items = lax.axis_index("items")
    user = lax.axis_index("users")
    z, y_hi, core = items // 4, lax.rem(items // 2, 2), lax.rem(items, 2)
    run = n // 4
    chip = (y_hi * 2 + z // run) * run + lax.rem(z, run)
    owners = 3 * run
    partner = {"items": items + 1 - 2 * core}
    per = n // GROUPS
    step = user // run
    order = (step + y_hi * (run - 1 - 2 * step)) * run + lax.rem(user, run)

    def at_chip(c):
        half = c // run
        z = lax.rem(half, 2) * run + lax.rem(c, run)
        return {"items": (z * 2 + half // 2) * 2 + core}

    def at_order(p):
        s = p // run
        return {"users": (s + y_hi * (run - 1 - 2 * s)) * run + lax.rem(p, run)}

    def others(me, start, stop, action, backwards=False):
        @pl.loop(start, stop)
        def _(i):
            p = start + stop - 1 - i if backwards else i

            @pl.when(p != me)
            def _():
                action(p)

    def send(src, dst, send_k, recv_sem, where):
        pltpu.make_async_remote_copy(
            src, dst, sem.at[send_k], recv_sem, device_id=where, device_id_type=MESH
        ).start()

    def part(ref, i, size=slots):
        return ref.at[pl.ds(pl.multiple_of(i * size, 8), size)]

    def wait(ref, count_rows, k):
        piece = ref.at[pl.ds(0, count_rows)]
        pltpu.make_async_copy(piece, piece, sem.at[k]).wait()

    barrier = pltpu.get_barrier_semaphore()
    loads = [pltpu.make_async_copy(inputs[i], local[i], load_sem.at[i]) for i in range(7)]
    for i in (4, 5, 6, 0, 1, 3, 2):
        loads[i].start()

    def greet(where):
        pl.semaphore_signal(barrier, inc=1, device_id=where, device_id_type=MESH)

    @pl.when(chip < owners)
    def _():
        others(chip, 0, n, lambda p: greet(at_chip(p)))

    greet(partner)

    @pl.loop(order + 1, n)
    def _(p):
        greet(at_order(p))

    place = lax.broadcasted_iota(I32, (8, width), 0) * width + lax.broadcasted_iota(I32, (8, width), 1)
    sub = lax.broadcasted_iota(I32, (slots, width), 0)
    for i in (4, 5, 6):
        loads[i].wait()
    mrow = jnp.zeros((8, width), I32)
    mcol = jnp.zeros((8, width), I32)
    colv = jnp.zeros((slots, width), I32)
    alive = count[0, 0]
    for t in range(slots):
        r, c = rows[0, 0, t], cols[0, 0, t]
        live = t < alive
        mrow = jnp.where(place == chip * slots + t, jnp.where(live, r, -1), mrow)
        mcol = jnp.where(place == user * slots + t, jnp.where(live, c, -1), mcol)
        colv = jnp.where(sub == t, c, colv)
    meta_r_out[...] = mrow
    meta_c_out[...] = mcol
    part(meta_r, chip, 8)[...] = mrow
    part(meta_c, user, 8)[...] = mcol

    loads[0].wait()
    hlen = hist.shape[1]
    bits = width.bit_length() - 1
    colw = jnp.concatenate([colv] * (hlen // width), axis=1) + items * item_blocks
    lane_id = lax.broadcasted_iota(I32, (width, hlen), 0)
    for q in range(n):
        h = hist[q : q + 1, :]
        block = lax.shift_right_logical(h, bits) == colw
        spot = (h & (width - 1)) == lane_id
        hits[pl.ds(q, slots, stride=n), :] = dot(
            jnp.where(block, 1.0, 0.0).astype(BF16), jnp.where(spot, 1.0, 0.0).astype(BF16), NT
        )

    loads[1].wait()
    loads[3].wait()

    for t in range(slots):
        degree = ideg[pl.ds(cols[0, 0, t], 1), :]
        high, low = halves(vals[t] * lax.rsqrt(degree.astype(F32)))
        vhi[t] = high
        vlo[t] = low
        h = hits[pl.ds(t * n, n), :].astype(BF16)
        msg1[pl.ds(t, n, stride=slots), :] = dot(h, high, NT) + dot(h, low, NT)

    pl.semaphore_wait(barrier, owners - (chip < owners).astype(I32) + order + 1)

    def forth(first, shift, recv, recv_k):
        def action(q):
            send(part(msg1, q), part(recv, chip), 5, sem.at[recv_k], at_chip(q - shift))

        others(chip + shift, first, first + run, action)

    others(chip, 0, owners, lambda p: send(meta_r_out, part(meta_r, chip, 8), 1, sem.at[2], at_chip(p)), True)
    forth(3 * run, run, recv1, 6)
    forth(0, 0, recv1, 6)
    forth(2 * run, 2 * run, recv1b, 13)
    forth(run, 0, recv1, 6)

    @pl.loop(0, order)
    def _(p):
        pl.semaphore_signal(ready, inc=1, device_id=at_order(p), device_id_type=MESH)

    def total(recv, recv_k, q, out_ref, in_ref, cross_k, msg, back_k):
        part(recv, chip)[...] = part(msg1, q)[...]
        wait(recv, slots * (n - 1), recv_k)
        high, low = halves(recv[...])
        acc = dot(pick_r[...], high) + dot(pick_r[...], low)
        out_ref[...] = acc
        cross = pltpu.make_async_remote_copy(
            out_ref, in_ref, sem.at[cross_k], sem.at[cross_k + 1], device_id=partner, device_id_type=MESH
        )
        cross.start()
        cross.wait()
        weights = (acc + in_ref[...]) / udeg[...].astype(F32)
        high, low = halves(weights)
        back = pick_rt[:, :user_blocks]
        msg[...] = dot(back, high) + dot(back, low)
        mine = back_sem.at[q // per]
        others(chip, 0, n, lambda p: send(part(msg, p), part(recv2, q), back_k, mine, at_chip(p)))
        part(recv2, q)[...] = part(msg, chip)[...]

    def gathered(ref):
        total = ref[0:8, :]
        for i in range(1, n):
            total = total + ref[8 * i : 8 * i + 8, :]
        return total

    loads[2].wait()

    @pl.when(chip < owners)
    def _():
        wait(meta_r, 8 * (n - 1), 2)
        ids = gathered(meta_r)
        block = lax.broadcasted_iota(I32, (width, width), 0)
        for k in range(span // width):
            at = slice(k * width, (k + 1) * width)
            hot = jnp.where(ids[k : k + 1, :] == block, 1.0, 0.0)
            pick_r[:, at] = hot[:user_blocks].astype(BF16)
            pick_rt[at, :] = hot.T.astype(BF16)
        first = chip + (chip // (2 * run)) * run
        total(recv1, 6, first, xsend, xrecv, 7, msg2, 9)

    @pl.when(chip < run)
    def _():
        total(recv1b, 13, chip + 2 * run, xsendb, xrecvb, 14, msg2b, 10)

    @pl.when(order < n - 1)
    def _():
        pl.semaphore_wait(ready, n - 1 - order)

    others(user, 0, n, lambda p: send(meta_c_out, part(meta_c, user, 8), 3, sem.at[4], {"users": p}))

    @pl.loop(0, GROUPS)
    def _(g):
        own = chip // per == jnp.where(g < 2, g, 2 * g - 4)
        for came, senders in ((own, per - 1), (jnp.logical_not(own), per)):

            @pl.when(came)
            def _():
                piece = recv2.at[pl.ds(0, slots * senders)]
                pltpu.make_async_copy(piece, piece, back_sem.at[g]).wait()

        for t in range(slots):
            spots = pl.ds(g * (per * slots) + t, per, stride=slots)
            high, low = halves(recv2[spots, :])
            msg3[spots, :] = dot(high, vhi[t]) + dot(low, vhi[t]) + dot(high, vlo[t])

        others(
            user, g * per, (g + 1) * per,
            lambda p: send(part(msg3, p), part(recv3, user), 11, sem.at[12], {"users": p}),
        )

    part(recv3, user)[...] = part(msg3, user)[...]
    wait(meta_c, 8 * (n - 1), 4)
    ids = gathered(meta_c)
    block = lax.broadcasted_iota(I32, (item_blocks, width), 0)
    for k in range(span // width):
        at = slice(k * width, (k + 1) * width)
        pick_c[:, at] = jnp.where(ids[k : k + 1, :] == block, 1.0, 0.0).astype(BF16)
    wait(recv3, slots * (n - 1), 12)
    high, low = halves(recv3[...])
    out[...] = dot(pick_c[...], high) + dot(pick_c[...], low)

    wait(meta_c, 8 * (n - 1), 3)
    wait(msg3, slots * (n - 1), 11)
    for here, queries_sent, ids_sent in (
        (chip < run, n - 2, owners - 1),
        ((chip >= run) & (chip < owners), n - 1, owners - 1),
        (chip >= owners, n, owners),
    ):

        @pl.when(here)
        def _():
            wait(meta_r, 8 * ids_sent, 1)
            wait(msg1, slots * queries_sent, 5)

    @pl.when(chip < owners)
    def _():
        wait(msg2, slots * (n - 1), 9)

    @pl.when(chip < run)
    def _():
        wait(msg2b, slots * (n - 1), 10)


def body(histories, item_degree, user_degree, tile_values, tile_rows, tile_cols, tile_count):
    queries = histories.shape[0]
    slots, width = tile_values.shape[2], tile_values.shape[-1]
    item_blocks = item_degree.shape[0] // width
    user_blocks = user_degree.shape[0] // width
    span = slots * queries
    vmem = pl.BlockSpec(memory_space=pltpu.VMEM)
    panel = pltpu.VMEM((span, width), F32)
    scores = pl.pallas_call(
        functools.partial(kernel, slots, queries, user_blocks, item_blocks, width),
        out_shape=jax.ShapeDtypeStruct((item_blocks, width), F32),
        in_specs=[pl.BlockSpec(memory_space=pltpu.HBM)] * 7,
        out_specs=vmem,
        scratch_shapes=[
            pltpu.VMEM(histories.shape, I32),
            pltpu.VMEM((item_blocks, width), I32),
            pltpu.VMEM((user_blocks, width), I32),
            pltpu.VMEM((slots, width, width), F32),
            pltpu.SMEM(tile_rows.shape, I32),
            pltpu.SMEM(tile_cols.shape, I32),
            pltpu.SMEM(tile_count.shape, I32),
            pltpu.VMEM((slots, width, width), BF16),
            pltpu.VMEM((slots, width, width), BF16),
            panel, panel, panel,
            pltpu.VMEM((user_blocks, width), F32),
            pltpu.VMEM((user_blocks, width), F32),
            panel, panel, panel, panel,
            panel,
            pltpu.VMEM((user_blocks, width), F32),
            pltpu.VMEM((user_blocks, width), F32),
            panel,
            pltpu.VMEM((8, width), I32),
            pltpu.VMEM((8 * queries, width), I32),
            pltpu.VMEM((8, width), I32),
            pltpu.VMEM((8 * queries, width), I32),
            pltpu.VMEM((user_blocks, span), BF16),
            pltpu.VMEM((span, width), BF16),
            pltpu.VMEM((item_blocks, span), BF16),
            pltpu.SemaphoreType.DMA((7,)),
            pltpu.SemaphoreType.DMA((GROUPS,)),
            pltpu.SemaphoreType.REGULAR,
            pltpu.SemaphoreType.DMA((16,)),
        ],
        compiler_params=pltpu.CompilerParams(
            collective_id=0, has_side_effects=True, vmem_limit_bytes=63 * 1024 * 1024
        ),
        cost_estimate=pl.CostEstimate(flops=10**8, bytes_accessed=4 * 10**6, transcendentals=0),
    )(
        histories,
        item_degree.reshape(item_blocks, width),
        user_degree.reshape(user_blocks, width),
        tile_values.reshape(slots, width, width),
        tile_rows, tile_cols, tile_count,
    )
    return scores.reshape(1, item_blocks * width)


def solution(mesh):
    in_specs = (
        P(),
        P("items"),
        P("users"),
        P("users", "items", None, None, None),
        P("users", "items", None),
        P("users", "items", None),
        P("users", "items"),
    )
    out_specs = P("users", "items")
    return jax.shard_map(body, mesh=mesh, in_specs=in_specs, out_specs=out_specs, check_vma=False)
```

```python
import functools

import jax
import jax.numpy as jnp
from jax import lax
from jax.experimental import pallas as pl
from jax.experimental.pallas import tpu as pltpu
from jax.sharding import PartitionSpec as P

MESH = pl.DeviceIdType.MESH
F32 = jnp.float32
BF16 = jnp.bfloat16
I32 = jnp.int32
NT = (((1,), (1,)), ((), ()))
NN = (((1,), (0,)), ((), ()))


def halves(x):
    high = x.astype(BF16)
    return high, (x - high.astype(F32)).astype(BF16)


def dot(a, b, dims=NN):
    return lax.dot_general(a, b, dims, preferred_element_type=F32)


OWNED = (0, 1, 4, 3, 8, 9, 11, 12, 2, 5, 7, 6, 13, 10, 15, 14)


def kernel(slots, queries, user_blocks, item_blocks, width, *refs):
    inputs, out, local = refs[:7], refs[7], refs[8:15]
    (
        vhi, vlo, hits, msg1, recv1, xsend, xrecv, msg2, recv2, msg3, recv3,
        meta_r_out, meta_r, meta_c_out, meta_c, pick_r, pick_rt, pick_c,
        load_sem, back_sem, sem,
    ) = refs[15:]
    hist, ideg, udeg, vals, rows, cols, count = local
    n = queries
    span = slots * n
    items = lax.axis_index("items")
    user = lax.axis_index("users")
    z, y_hi, core = items // 4, lax.rem(items // 2, 2), lax.rem(items, 2)
    depth, run = n // 2, n // 4
    partner = {"items": items + 1 - 2 * core}

    def chip_of(z, y):
        return ((z // run) * 2 + y) * run + lax.rem(z, run)

    chip = chip_of(z, y_hi)

    owned = OWNED if n == len(OWNED) else tuple(range(n))

    away = [(dz, dy) for dz in range(depth) for dy in range(2) if dz or dy]
    away.sort(key=lambda d: -min(d[0], depth - d[0]) - 4 * d[1])

    def chips(action):
        for dz, dy in away:
            there, y = lax.rem(z + dz, depth), lax.rem(y_hi + dy, 2)
            action(chip_of(there, y), {"items": (there * 2 + y) * 2 + core})

    def users(action):
        @pl.loop(1, n)
        def _(i):
            action(lax.rem(user + i, n))

    def send(src, dst, send_k, recv_sem, where):
        pltpu.make_async_remote_copy(
            src, dst, sem.at[send_k], recv_sem, device_id=where, device_id_type=MESH
        ).start()

    def part(ref, i, size=slots):
        return ref.at[pl.ds(pl.multiple_of(i * size, 8), size)]

    def wait(ref, count_rows, k):
        piece = ref.at[pl.ds(0, count_rows)]
        pltpu.make_async_copy(piece, piece, sem.at[k]).wait()

    barrier = pltpu.get_barrier_semaphore()
    loads = [pltpu.make_async_copy(inputs[i], local[i], load_sem.at[i]) for i in range(7)]
    for i in (4, 5, 6, 0, 1, 3, 2):
        loads[i].start()

    def greet(where):
        pl.semaphore_signal(barrier, inc=1, device_id=where, device_id_type=MESH)

    chips(lambda c, where: greet(where))
    users(lambda p: greet({"users": p}))
    greet(partner)

    lane = lax.broadcasted_iota(I32, (1, width), 1)
    sub = lax.broadcasted_iota(I32, (slots, width), 0)
    for i in (4, 5, 6):
        loads[i].wait()
    mrow = jnp.zeros((1, width), I32)
    mcol = jnp.zeros((1, width), I32)
    colv = jnp.zeros((slots, width), I32)
    alive = count[0, 0]
    for t in range(slots):
        r, c = rows[0, 0, t], cols[0, 0, t]
        live = t < alive
        mrow = jnp.where(lane == lax.rem(chip * slots + t, width), jnp.where(live, r, -1), mrow)
        mcol = jnp.where(lane == lax.rem(user * slots + t, width), jnp.where(live, c, -1), mcol)
        colv = jnp.where(sub == t, c, colv)
    meta_r_out[...] = mrow
    meta_c_out[...] = mcol
    meta_r[chip] = mrow
    meta_c[user] = mcol

    loads[0].wait()
    hlen = hist.shape[1]
    bits = width.bit_length() - 1
    colw = jnp.concatenate([colv] * (hlen // width), axis=1) + items * item_blocks
    lane_id = lax.broadcasted_iota(I32, (width, hlen), 0)
    for q in range(n):
        h = hist[q : q + 1, :]
        block = lax.shift_right_logical(h, bits) == colw
        spot = (h & (width - 1)) == lane_id
        hits[pl.ds(owned.index(q), slots, stride=n), :] = dot(
            jnp.where(block, 1.0, 0.0).astype(BF16), jnp.where(spot, 1.0, 0.0).astype(BF16), NT
        )

    loads[1].wait()
    loads[3].wait()

    for t in range(slots):
        degree = ideg[pl.ds(cols[0, 0, t], 1), :]
        high, low = halves(vals[t] * lax.rsqrt(degree.astype(F32)))
        vhi[t] = high
        vlo[t] = low
        h = hits[pl.ds(t * n, n), :].astype(BF16)
        msg1[pl.ds(t, n, stride=slots), :] = dot(h, high, NT) + dot(h, low, NT)

    pl.semaphore_wait(barrier, 2 * (n - 1) + 1)

    def forth(c, where):
        send(meta_r_out, meta_r.at[chip], 1, sem.at[2], where)
        send(part(msg1, c), part(recv1, chip), 5, sem.at[6], where)

    chips(forth)
    part(recv1, chip)[...] = part(msg1, chip)[...]
    users(lambda p: send(meta_c_out, meta_c.at[user], 3, sem.at[4], {"users": p}))

    def gathered(ref, k):
        ids = jnp.zeros((1, width), I32)
        for i in range(k * width // slots, min(n, -(-(k + 1) * width // slots))):
            from_i = (lane >= i * slots - k * width) & (lane < (i + 1) * slots - k * width)
            ids = jnp.where(from_i, ref[i], ids)
        return ids

    wait(meta_r, n - 1, 2)
    block = lax.broadcasted_iota(I32, (width, width), 0)
    for k in range(span // width):
        at = slice(k * width, (k + 1) * width)
        hot = jnp.where(gathered(meta_r, k) == block, 1.0, 0.0)
        pick_r[:, at] = hot[:user_blocks].astype(BF16)
        pick_rt[at, :] = hot.T.astype(BF16)

    wait(recv1, slots * (n - 1), 6)
    high, low = halves(recv1[...])
    acc = dot(pick_r[...], high) + dot(pick_r[...], low)
    xsend[...] = acc
    cross = pltpu.make_async_remote_copy(
        xsend, xrecv, sem.at[7], sem.at[8], device_id=partner, device_id_type=MESH
    )
    cross.start()
    cross.wait()
    loads[2].wait()
    weights = (acc + xrecv[...]) / udeg[...].astype(F32)
    high, low = halves(weights)
    back = pick_rt[:, :user_blocks]
    msg2[...] = dot(back, high) + dot(back, low)
    mine = back_sem.at[chip // run]
    chips(lambda c, where: send(part(msg2, c), part(recv2, chip), 9, mine, where))
    part(recv2, chip)[...] = part(msg2, chip)[...]

    @pl.loop(0, 4)
    def _(j):
        g = lax.rem(z // run + lax.rem(j, 2), 2) * 2 + lax.rem(y_hi + j // 2, 2)
        for came, senders in ((j == 0, run - 1), (j > 0, run)):

            @pl.when(came)
            def _():
                piece = recv2.at[pl.ds(0, slots * senders)]
                pltpu.make_async_copy(piece, piece, back_sem.at[g]).wait()

        for t in range(slots):
            spots = pl.ds(g * (run * slots) + t, run, stride=slots)
            high, low = halves(recv2[spots, :])
            msg3[spots, :] = dot(high, vhi[t]) + dot(low, vhi[t]) + dot(high, vlo[t])

        for m in range(run):
            c, u = g * run + m, owned[m]
            for k in range(1, 4):
                u = jnp.where(g == k, owned[k * run + m], u)

            @pl.when(u != user)
            def _():
                send(part(msg3, c), part(recv3, user), 11, sem.at[12], {"users": u})

    own = 0
    for c in range(1, n):
        own = jnp.where(user == owned[c], c, own)
    part(recv3, user)[...] = part(msg3, own)[...]
    wait(meta_c, n - 1, 4)
    block = lax.broadcasted_iota(I32, (item_blocks, width), 0)
    for k in range(span // width):
        at = slice(k * width, (k + 1) * width)
        pick_c[:, at] = jnp.where(gathered(meta_c, k) == block, 1.0, 0.0).astype(BF16)
    wait(recv3, slots * (n - 1), 12)
    high, low = halves(recv3[...])
    out[...] = dot(pick_c[...], high) + dot(pick_c[...], low)

    wait(meta_r, n - 1, 1)
    wait(meta_c, n - 1, 3)
    wait(msg1, slots * (n - 1), 5)
    wait(msg2, slots * (n - 1), 9)
    wait(msg3, slots * (n - 1), 11)


def body(histories, item_degree, user_degree, tile_values, tile_rows, tile_cols, tile_count):
    queries = histories.shape[0]
    slots, width = tile_values.shape[2], tile_values.shape[-1]
    item_blocks = item_degree.shape[0] // width
    user_blocks = user_degree.shape[0] // width
    span = slots * queries
    vmem = pl.BlockSpec(memory_space=pltpu.VMEM)
    panel = pltpu.VMEM((span, width), F32)
    scores = pl.pallas_call(
        functools.partial(kernel, slots, queries, user_blocks, item_blocks, width),
        out_shape=jax.ShapeDtypeStruct((item_blocks, width), F32),
        in_specs=[pl.BlockSpec(memory_space=pltpu.HBM)] * 7,
        out_specs=vmem,
        scratch_shapes=[
            pltpu.VMEM(histories.shape, I32),
            pltpu.VMEM((item_blocks, width), I32),
            pltpu.VMEM((user_blocks, width), I32),
            pltpu.VMEM((slots, width, width), F32),
            pltpu.SMEM(tile_rows.shape, I32),
            pltpu.SMEM(tile_cols.shape, I32),
            pltpu.SMEM(tile_count.shape, I32),
            pltpu.VMEM((slots, width, width), BF16),
            pltpu.VMEM((slots, width, width), BF16),
            panel, panel, panel,
            pltpu.VMEM((user_blocks, width), F32),
            pltpu.VMEM((user_blocks, width), F32),
            panel, panel, panel, panel,
            pltpu.VMEM((1, width), I32),
            pltpu.VMEM((queries, 1, width), I32),
            pltpu.VMEM((1, width), I32),
            pltpu.VMEM((queries, 1, width), I32),
            pltpu.VMEM((user_blocks, span), BF16),
            pltpu.VMEM((span, width), BF16),
            pltpu.VMEM((item_blocks, span), BF16),
            pltpu.SemaphoreType.DMA((7,)),
            pltpu.SemaphoreType.DMA((4,)),
            pltpu.SemaphoreType.DMA((13,)),
        ],
        compiler_params=pltpu.CompilerParams(
            collective_id=0, has_side_effects=True, vmem_limit_bytes=32 * 1024 * 1024
        ),
        cost_estimate=pl.CostEstimate(flops=10**8, bytes_accessed=4 * 10**6, transcendentals=0),
    )(*[pltpu.with_memory_space_constraint(x, pltpu.HBM) for x in (
        histories,
        item_degree.reshape(item_blocks, width),
        user_degree.reshape(user_blocks, width),
        tile_values.reshape(slots, width, width),
        tile_rows, tile_cols,
    )], tile_count)
    return scores.reshape(1, item_blocks * width)


def solution(mesh):
    in_specs = (
        P(),
        P("items"),
        P("users"),
        P("users", "items", None, None, None),
        P("users", "items", None),
        P("users", "items", None),
        P("users", "items"),
    )
    out_specs = P("users", "items")
    return jax.shard_map(body, mesh=mesh, in_specs=in_specs, out_specs=out_specs, check_vma=False)
```

```python
import functools

import jax
import jax.numpy as jnp
from jax import lax
from jax.experimental import pallas as pl
from jax.experimental.pallas import tpu as pltpu
from jax.sharding import PartitionSpec as P

MESH = pl.DeviceIdType.MESH
F32 = jnp.float32
BF16 = jnp.bfloat16
I32 = jnp.int32
NT = (((1,), (1,)), ((), ()))
NN = (((1,), (0,)), ((), ()))


def halves(x):
    high = x.astype(BF16)
    return high, (x - high.astype(F32)).astype(BF16)


def dot(a, b, dims=NN):
    return lax.dot_general(a, b, dims, preferred_element_type=F32)


OWNED = (0, 1, 4, 3, 8, 9, 11, 12, 2, 5, 7, 6, 13, 10, 15, 14)


PIECE = 4


def kernel(slots, queries, user_blocks, item_blocks, width, *refs):
    inputs, out, local = refs[:7], refs[7], refs[8:15]
    (
        vhi, vlo, hits, msg1, recv1, xsend, xrecv, msg2, recv2, msg3, recv3,
        meta_r_out, meta_r, meta_c_out, meta_c, pick_r, pick_rt, pick_c,
        load_sem, vals_sem, back_sem, sem,
    ) = refs[15:]
    hist, ideg, udeg, vals, rows, cols, count = local
    n = queries
    span = slots * n
    items = lax.axis_index("items")
    user = lax.axis_index("users")
    z, y_hi, core = items // 4, lax.rem(items // 2, 2), lax.rem(items, 2)
    depth, run = n // 2, n // 4
    partner = {"items": items + 1 - 2 * core}

    def chip_of(z, y):
        return ((z // run) * 2 + y) * run + lax.rem(z, run)

    chip = chip_of(z, y_hi)

    owned = OWNED if n == len(OWNED) else tuple(range(n))

    away = [(dz, dy) for dz in range(depth) for dy in range(2) if dz or dy]
    away.sort(key=lambda d: -min(d[0], depth - d[0]) - 10 * d[1])

    def chips(action):
        for dz, dy in away:
            there, y = lax.rem(z + dz, depth), lax.rem(y_hi + dy, 2)
            action(chip_of(there, y), {"items": (there * 2 + y) * 2 + core})

    def users(action):
        @pl.loop(1, n)
        def _(i):
            action(lax.rem(user + i, n))

    def send(src, dst, send_k, recv_sem, where):
        pltpu.make_async_remote_copy(
            src, dst, sem.at[send_k], recv_sem, device_id=where, device_id_type=MESH
        ).start()

    def part(ref, i, size=slots):
        return ref.at[pl.ds(pl.multiple_of(i * size, 8), size)]

    def wait(ref, count_rows, k):
        piece = ref.at[pl.ds(0, count_rows)]
        pltpu.make_async_copy(piece, piece, sem.at[k]).wait()

    barrier = pltpu.get_barrier_semaphore()
    loads = {i: pltpu.make_async_copy(inputs[i], local[i], load_sem.at[i]) for i in (0, 1, 2, 4, 5, 6)}
    pieces = []
    for i in range(0, slots, PIECE):
        here = pl.ds(i, PIECE)
        pieces.append(pltpu.make_async_copy(inputs[3].at[here], vals.at[here], vals_sem.at[i // PIECE]))
    for load in (loads[4], loads[5], loads[6], loads[0], loads[1], *pieces, loads[2]):
        load.start()

    def greet(where):
        pl.semaphore_signal(barrier, inc=1, device_id=where, device_id_type=MESH)

    chips(lambda c, where: greet(where))
    users(lambda p: greet({"users": p}))
    greet(partner)

    lane = lax.broadcasted_iota(I32, (1, width), 1)
    sub = lax.broadcasted_iota(I32, (slots, width), 0)
    for i in (4, 5, 6):
        loads[i].wait()
    mrow = jnp.zeros((1, width), I32)
    mcol = jnp.zeros((1, width), I32)
    colv = jnp.zeros((slots, width), I32)
    alive = count[0, 0]
    for t in range(slots):
        r, c = rows[0, 0, t], cols[0, 0, t]
        live = t < alive
        mrow = jnp.where(lane == lax.rem(chip * slots + t, width), jnp.where(live, r, -1), mrow)
        mcol = jnp.where(lane == lax.rem(user * slots + t, width), jnp.where(live, c, -1), mcol)
        colv = jnp.where(sub == t, c, colv)
    meta_r_out[...] = mrow
    meta_c_out[...] = mcol
    meta_r[chip] = mrow
    meta_c[user] = mcol

    loads[0].wait()
    hlen = hist.shape[1]
    bits = width.bit_length() - 1
    colw = jnp.concatenate([colv] * (hlen // width), axis=1) + items * item_blocks
    lane_id = lax.broadcasted_iota(I32, (width, hlen), 0)
    for q in range(n):
        h = hist[q : q + 1, :]
        block = lax.shift_right_logical(h, bits) == colw
        spot = (h & (width - 1)) == lane_id
        hits[pl.ds(owned.index(q), slots, stride=n), :] = dot(
            jnp.where(block, 1.0, 0.0).astype(BF16), jnp.where(spot, 1.0, 0.0).astype(BF16), NT
        )

    loads[1].wait()

    for t in range(slots):
        if t % PIECE == 0:
            pieces[t // PIECE].wait()
        degree = ideg[pl.ds(cols[0, 0, t], 1), :]
        high, low = halves(vals[t] * lax.rsqrt(degree.astype(F32)))
        vhi[t] = high
        vlo[t] = low
        h = hits[pl.ds(t * n, n), :].astype(BF16)
        msg1[pl.ds(t, n, stride=slots), :] = dot(h, high, NT) + dot(h, low, NT)

    pl.semaphore_wait(barrier, 2 * (n - 1) + 1)

    def forth(c, where):
        send(meta_r_out, meta_r.at[chip], 1, sem.at[2], where)
        send(part(msg1, c), part(recv1, chip), 5, sem.at[6], where)

    chips(forth)
    part(recv1, chip)[...] = part(msg1, chip)[...]
    users(lambda p: send(meta_c_out, meta_c.at[user], 3, sem.at[4], {"users": p}))

    def gathered(ref, k):
        ids = jnp.zeros((1, width), I32)
        for i in range(k * width // slots, min(n, -(-(k + 1) * width // slots))):
            from_i = (lane >= i * slots - k * width) & (lane < (i + 1) * slots - k * width)
            ids = jnp.where(from_i, ref[i], ids)
        return ids

    wait(meta_r, n - 1, 2)
    block = lax.broadcasted_iota(I32, (width, width), 0)
    for k in range(span // width):
        at = slice(k * width, (k + 1) * width)
        pick_r[:, at] = jnp.where(gathered(meta_r, k) == block[:user_blocks], 1.0, 0.0).astype(BF16)

    wait(recv1, slots * (n - 1), 6)
    high, low = halves(recv1[...])
    acc = dot(pick_r[...], high) + dot(pick_r[...], low)
    xsend[...] = acc
    cross = pltpu.make_async_remote_copy(
        xsend, xrecv, sem.at[7], sem.at[8], device_id=partner, device_id_type=MESH
    )
    cross.start()
    for k in range(span // width):
        hot = jnp.where(gathered(meta_r, k) == block, 1.0, 0.0)
        pick_rt[k * width : (k + 1) * width, :] = hot.T.astype(BF16)
    loads[2].wait()
    cross.wait()
    weights = (acc + xrecv[...]) / udeg[...].astype(F32)
    high, low = halves(weights)
    back = pick_rt[:, :user_blocks]
    msg2[...] = dot(back, high) + dot(back, low)
    mine = back_sem.at[chip // run]
    chips(lambda c, where: send(part(msg2, c), part(recv2, chip), 9, mine, where))
    part(recv2, chip)[...] = part(msg2, chip)[...]

    @pl.loop(0, 4)
    def _(j):
        g = lax.rem(z // run + lax.rem(j, 2), 2) * 2 + lax.rem(y_hi + j // 2, 2)
        for came, senders in ((j == 0, run - 1), (j > 0, run)):

            @pl.when(came)
            def _():
                piece = recv2.at[pl.ds(0, slots * senders)]
                pltpu.make_async_copy(piece, piece, back_sem.at[g]).wait()

        for t in range(slots):
            spots = pl.ds(g * (run * slots) + t, run, stride=slots)
            x = recv2[spots, :]
            high = x.astype(BF16).astype(F32)
            x = jnp.concatenate([high, x - high], axis=0).astype(BF16)
            y = dot(x, vhi[t]) + dot(x, vlo[t])
            msg3[spots, :] = y[:run] + y[run:]

        for m in range(run):
            c, u = g * run + m, owned[m]
            for k in range(1, 4):
                u = jnp.where(g == k, owned[k * run + m], u)

            @pl.when(u != user)
            def _():
                send(part(msg3, c), part(recv3, user), 11, sem.at[12], {"users": u})

    own = 0
    for c in range(1, n):
        own = jnp.where(user == owned[c], c, own)
    part(recv3, user)[...] = part(msg3, own)[...]
    wait(meta_c, n - 1, 4)
    block = lax.broadcasted_iota(I32, (item_blocks, width), 0)
    for k in range(span // width):
        at = slice(k * width, (k + 1) * width)
        pick_c[:, at] = jnp.where(gathered(meta_c, k) == block, 1.0, 0.0).astype(BF16)
    wait(recv3, slots * (n - 1), 12)
    high, low = halves(recv3[...])
    out[...] = dot(pick_c[...], high) + dot(pick_c[...], low)

    wait(meta_r, n - 1, 1)
    wait(meta_c, n - 1, 3)
    wait(msg1, slots * (n - 1), 5)
    wait(msg2, slots * (n - 1), 9)
    wait(msg3, slots * (n - 1), 11)


def body(histories, item_degree, user_degree, tile_values, tile_rows, tile_cols, tile_count):
    queries = histories.shape[0]
    slots, width = tile_values.shape[2], tile_values.shape[-1]
    item_blocks = item_degree.shape[0] // width
    user_blocks = user_degree.shape[0] // width
    span = slots * queries
    vmem = pl.BlockSpec(memory_space=pltpu.VMEM)
    panel = pltpu.VMEM((span, width), F32)
    scores = pl.pallas_call(
        functools.partial(kernel, slots, queries, user_blocks, item_blocks, width),
        out_shape=jax.ShapeDtypeStruct((item_blocks, width), F32),
        in_specs=[pl.BlockSpec(memory_space=pltpu.HBM)] * 7,
        out_specs=vmem,
        scratch_shapes=[
            pltpu.VMEM(histories.shape, I32),
            pltpu.VMEM((item_blocks, width), I32),
            pltpu.VMEM((user_blocks, width), I32),
            pltpu.VMEM((slots, width, width), F32),
            pltpu.SMEM(tile_rows.shape, I32),
            pltpu.SMEM(tile_cols.shape, I32),
            pltpu.SMEM(tile_count.shape, I32),
            pltpu.VMEM((slots, width, width), BF16),
            pltpu.VMEM((slots, width, width), BF16),
            panel, panel, panel,
            pltpu.VMEM((user_blocks, width), F32),
            pltpu.VMEM((user_blocks, width), F32),
            panel, panel, panel, panel,
            pltpu.VMEM((1, width), I32),
            pltpu.VMEM((queries, 1, width), I32),
            pltpu.VMEM((1, width), I32),
            pltpu.VMEM((queries, 1, width), I32),
            pltpu.VMEM((user_blocks, span), BF16),
            pltpu.VMEM((span, width), BF16),
            pltpu.VMEM((item_blocks, span), BF16),
            pltpu.SemaphoreType.DMA((7,)),
            pltpu.SemaphoreType.DMA((slots // PIECE,)),
            pltpu.SemaphoreType.DMA((4,)),
            pltpu.SemaphoreType.DMA((13,)),
        ],
        compiler_params=pltpu.CompilerParams(
            collective_id=0, has_side_effects=True, vmem_limit_bytes=32 * 1024 * 1024
        ),
        cost_estimate=pl.CostEstimate(flops=10**8, bytes_accessed=4 * 10**6, transcendentals=0),
    )(*[pltpu.with_memory_space_constraint(x, pltpu.HBM) for x in (
        histories,
        item_degree.reshape(item_blocks, width),
        user_degree.reshape(user_blocks, width),
        tile_values.reshape(slots, width, width),
        tile_rows, tile_cols,
    )], tile_count)
    return scores.reshape(1, item_blocks * width)


def solution(mesh):
    in_specs = (
        P(),
        P("items"),
        P("users"),
        P("users", "items", None, None, None),
        P("users", "items", None),
        P("users", "items", None),
        P("users", "items"),
    )
    out_specs = P("users", "items")
    return jax.shard_map(body, mesh=mesh, in_specs=in_specs, out_specs=out_specs, check_vma=False)
```

```python
import functools

import jax
import jax.numpy as jnp
from jax import lax
from jax.experimental import pallas as pl
from jax.experimental.pallas import tpu as pltpu
from jax.sharding import PartitionSpec as P

MESH = pl.DeviceIdType.MESH
F32 = jnp.float32
BF16 = jnp.bfloat16
I32 = jnp.int32
NT = (((1,), (1,)), ((), ()))
NN = (((1,), (0,)), ((), ()))


def halves(x):
    high = x.astype(BF16)
    return high, (x - high.astype(F32)).astype(BF16)


def dot(a, b, dims=NN):
    return lax.dot_general(a, b, dims, preferred_element_type=F32)


OWNED = (0, 1, 4, 3, 8, 9, 11, 12, 2, 5, 7, 6, 13, 10, 15, 14)


def select(hot, x):
    wide = x.shape[1]
    y = dot(hot, jnp.concatenate(halves(x), axis=1))
    return y[:, :wide] + y[:, wide:]


PIECE = 4


def kernel(slots, queries, user_blocks, item_blocks, width, *refs):
    inputs, out, local = refs[:7], refs[7], refs[8:15]
    (
        vhi, vlo, hits, msg1, recv1, xsend, xrecv, msg2, recv2, msg3, recv3,
        meta_r_out, meta_r, meta_c_out, meta_c, pick_r, pick_rt, pick_c,
        load_sem, vals_sem, back_sem, sem,
    ) = refs[15:]
    hist, ideg, udeg, vals, rows, cols, count = local
    n = queries
    span = slots * n
    items = lax.axis_index("items")
    user = lax.axis_index("users")
    z, y_hi, core = items // 4, lax.rem(items // 2, 2), lax.rem(items, 2)
    depth, run = n // 2, n // 4
    partner = {"items": items + 1 - 2 * core}

    def chip_of(z, y):
        return ((z // run) * 2 + y) * run + lax.rem(z, run)

    chip = chip_of(z, y_hi)

    owned = OWNED if n == len(OWNED) else tuple(range(n))

    away = [(dz, dy) for dz in range(depth) for dy in range(2) if dz or dy]
    away.sort(key=lambda d: -min(d[0], depth - d[0]) - 10 * d[1])

    def chips(action):
        for dz, dy in away:
            there, y = lax.rem(z + dz, depth), lax.rem(y_hi + dy, 2)
            action(chip_of(there, y), {"items": (there * 2 + y) * 2 + core})

    def users(action):
        @pl.loop(1, n)
        def _(i):
            action(lax.rem(user + i, n))

    def send(src, dst, send_k, recv_sem, where):
        pltpu.make_async_remote_copy(
            src, dst, sem.at[send_k], recv_sem, device_id=where, device_id_type=MESH
        ).start()

    def part(ref, i, size=slots):
        return ref.at[pl.ds(pl.multiple_of(i * size, 8), size)]

    def wait(ref, count_rows, k):
        piece = ref.at[pl.ds(0, count_rows)]
        pltpu.make_async_copy(piece, piece, sem.at[k]).wait()

    barrier = pltpu.get_barrier_semaphore()
    loads = {i: pltpu.make_async_copy(inputs[i], local[i], load_sem.at[i]) for i in (0, 1, 2, 4, 5, 6)}
    pieces = []
    for i in range(0, slots, PIECE):
        here = pl.ds(i, PIECE)
        pieces.append(pltpu.make_async_copy(inputs[3].at[here], vals.at[here], vals_sem.at[i // PIECE]))
    for load in (loads[4], loads[5], loads[6], loads[0], loads[1], *pieces, loads[2]):
        load.start()

    def greet(where):
        pl.semaphore_signal(barrier, inc=1, device_id=where, device_id_type=MESH)

    chips(lambda c, where: greet(where))
    users(lambda p: greet({"users": p}))
    greet(partner)

    lane = lax.broadcasted_iota(I32, (1, width), 1)
    sub = lax.broadcasted_iota(I32, (slots, width), 0)
    for i in (4, 5, 6):
        loads[i].wait()
    mrow = jnp.zeros((1, width), I32)
    mcol = jnp.zeros((1, width), I32)
    colv = jnp.zeros((slots, width), I32)
    alive = count[0, 0]
    for t in range(slots):
        r, c = rows[0, 0, t], cols[0, 0, t]
        live = t < alive
        mrow = jnp.where(lane == lax.rem(chip * slots + t, width), jnp.where(live, r, -1), mrow)
        mcol = jnp.where(lane == lax.rem(user * slots + t, width), jnp.where(live, c, -1), mcol)
        colv = jnp.where(sub == t, c, colv)
    meta_r_out[...] = mrow
    meta_c_out[...] = mcol
    meta_r[chip] = mrow
    meta_c[user] = mcol

    loads[0].wait()
    hlen = hist.shape[1]
    bits = width.bit_length() - 1
    colw = jnp.concatenate([colv] * (hlen // width), axis=1) + items * item_blocks
    lane_id = lax.broadcasted_iota(I32, (width, hlen), 0)
    for q in range(n):
        h = hist[q : q + 1, :]
        block = lax.shift_right_logical(h, bits) == colw
        spot = (h & (width - 1)) == lane_id
        hits[pl.ds(owned.index(q), slots, stride=n), :] = dot(
            jnp.where(block, 1.0, 0.0).astype(BF16), jnp.where(spot, 1.0, 0.0).astype(BF16), NT
        )

    loads[1].wait()

    for t in range(slots):
        if t % PIECE == 0:
            pieces[t // PIECE].wait()
        degree = ideg[pl.ds(cols[0, 0, t], 1), :]
        high, low = halves(vals[t] * lax.rsqrt(degree.astype(F32)))
        vhi[t] = high
        vlo[t] = low
        h = hits[pl.ds(t * n, n), :].astype(BF16)
        msg1[pl.ds(t, n, stride=slots), :] = dot(h, high, NT) + dot(h, low, NT)

    pl.semaphore_wait(barrier, 2 * (n - 1) + 1)

    def forth(c, where):
        send(meta_r_out, meta_r.at[chip], 1, sem.at[2], where)
        send(part(msg1, c), part(recv1, chip), 5, sem.at[6], where)

    chips(forth)
    part(recv1, chip)[...] = part(msg1, chip)[...]
    users(lambda p: send(meta_c_out, meta_c.at[user], 3, sem.at[4], {"users": p}))

    def gathered(ref, k):
        ids = jnp.zeros((1, width), I32)
        for i in range(k * width // slots, min(n, -(-(k + 1) * width // slots))):
            from_i = (lane >= i * slots - k * width) & (lane < (i + 1) * slots - k * width)
            ids = jnp.where(from_i, ref[i], ids)
        return ids

    wait(meta_r, n - 1, 2)
    block = lax.broadcasted_iota(I32, (width, width), 0)
    for k in range(span // width):
        at = slice(k * width, (k + 1) * width)
        pick_r[:, at] = jnp.where(gathered(meta_r, k) == block[:user_blocks], 1.0, 0.0).astype(BF16)

    wait(recv1, slots * (n - 1), 6)
    acc = select(pick_r[...], recv1[...])
    xsend[...] = acc
    cross = pltpu.make_async_remote_copy(
        xsend, xrecv, sem.at[7], sem.at[8], device_id=partner, device_id_type=MESH
    )
    cross.start()
    for k in range(span // width):
        hot = jnp.where(gathered(meta_r, k) == block, 1.0, 0.0)
        pick_rt[k * width : (k + 1) * width, :] = hot.T.astype(BF16)
    loads[2].wait()
    cross.wait()
    weights = (acc + xrecv[...]) / udeg[...].astype(F32)
    msg2[...] = select(pick_rt[:, :user_blocks], weights)
    mine = back_sem.at[chip // run]
    chips(lambda c, where: send(part(msg2, c), part(recv2, chip), 9, mine, where))
    part(recv2, chip)[...] = part(msg2, chip)[...]

    @pl.loop(0, 4)
    def _(j):
        g = lax.rem(z // run + lax.rem(j, 2), 2) * 2 + lax.rem(y_hi + j // 2, 2)
        for came, senders in ((j == 0, run - 1), (j > 0, run)):

            @pl.when(came)
            def _():
                piece = recv2.at[pl.ds(0, slots * senders)]
                pltpu.make_async_copy(piece, piece, back_sem.at[g]).wait()

        for t in range(slots):
            spots = pl.ds(g * (run * slots) + t, run, stride=slots)
            x = recv2[spots, :]
            high = x.astype(BF16).astype(F32)
            x = jnp.concatenate([high, x - high], axis=0).astype(BF16)
            y = dot(x, vhi[t]) + dot(x, vlo[t])
            msg3[spots, :] = y[:run] + y[run:]

        for m in range(run):
            c, u = g * run + m, owned[m]
            for k in range(1, 4):
                u = jnp.where(g == k, owned[k * run + m], u)

            @pl.when(u != user)
            def _():
                send(part(msg3, c), part(recv3, user), 11, sem.at[12], {"users": u})

    own = 0
    for c in range(1, n):
        own = jnp.where(user == owned[c], c, own)
    part(recv3, user)[...] = part(msg3, own)[...]
    wait(meta_c, n - 1, 4)
    block = lax.broadcasted_iota(I32, (item_blocks, width), 0)
    for k in range(span // width):
        at = slice(k * width, (k + 1) * width)
        pick_c[:, at] = jnp.where(gathered(meta_c, k) == block, 1.0, 0.0).astype(BF16)
    wait(recv3, slots * (n - 1), 12)
    out[...] = select(pick_c[...], recv3[...])

    wait(meta_r, n - 1, 1)
    wait(meta_c, n - 1, 3)
    wait(msg1, slots * (n - 1), 5)
    wait(msg2, slots * (n - 1), 9)
    wait(msg3, slots * (n - 1), 11)


def body(histories, item_degree, user_degree, tile_values, tile_rows, tile_cols, tile_count):
    queries = histories.shape[0]
    slots, width = tile_values.shape[2], tile_values.shape[-1]
    item_blocks = item_degree.shape[0] // width
    user_blocks = user_degree.shape[0] // width
    span = slots * queries
    vmem = pl.BlockSpec(memory_space=pltpu.VMEM)
    panel = pltpu.VMEM((span, width), F32)
    scores = pl.pallas_call(
        functools.partial(kernel, slots, queries, user_blocks, item_blocks, width),
        out_shape=jax.ShapeDtypeStruct((item_blocks, width), F32),
        in_specs=[pl.BlockSpec(memory_space=pltpu.HBM)] * 7,
        out_specs=vmem,
        scratch_shapes=[
            pltpu.VMEM(histories.shape, I32),
            pltpu.VMEM((item_blocks, width), I32),
            pltpu.VMEM((user_blocks, width), I32),
            pltpu.VMEM((slots, width, width), F32),
            pltpu.SMEM(tile_rows.shape, I32),
            pltpu.SMEM(tile_cols.shape, I32),
            pltpu.SMEM(tile_count.shape, I32),
            pltpu.VMEM((slots, width, width), BF16),
            pltpu.VMEM((slots, width, width), BF16),
            panel, panel, panel,
            pltpu.VMEM((user_blocks, width), F32),
            pltpu.VMEM((user_blocks, width), F32),
            panel, panel, panel, panel,
            pltpu.VMEM((1, width), I32),
            pltpu.VMEM((queries, 1, width), I32),
            pltpu.VMEM((1, width), I32),
            pltpu.VMEM((queries, 1, width), I32),
            pltpu.VMEM((user_blocks, span), BF16),
            pltpu.VMEM((span, width), BF16),
            pltpu.VMEM((item_blocks, span), BF16),
            pltpu.SemaphoreType.DMA((7,)),
            pltpu.SemaphoreType.DMA((slots // PIECE,)),
            pltpu.SemaphoreType.DMA((4,)),
            pltpu.SemaphoreType.DMA((13,)),
        ],
        compiler_params=pltpu.CompilerParams(
            collective_id=0, has_side_effects=True, vmem_limit_bytes=32 * 1024 * 1024
        ),
        cost_estimate=pl.CostEstimate(flops=10**8, bytes_accessed=4 * 10**6, transcendentals=0),
    )(*[pltpu.with_memory_space_constraint(x, pltpu.HBM) for x in (
        histories,
        item_degree.reshape(item_blocks, width),
        user_degree.reshape(user_blocks, width),
        tile_values.reshape(slots, width, width),
        tile_rows, tile_cols,
    )], tile_count)
    return scores.reshape(1, item_blocks * width)


def solution(mesh):
    in_specs = (
        P(),
        P("items"),
        P("users"),
        P("users", "items", None, None, None),
        P("users", "items", None),
        P("users", "items", None),
        P("users", "items"),
    )
    out_specs = P("users", "items")
    return jax.shard_map(body, mesh=mesh, in_specs=in_specs, out_specs=out_specs, check_vma=False)
```

```python
import functools

import jax
import jax.numpy as jnp
from jax import lax
from jax.experimental import pallas as pl
from jax.experimental.pallas import tpu as pltpu
from jax.sharding import PartitionSpec as P

MESH = pl.DeviceIdType.MESH
F32 = jnp.float32
BF16 = jnp.bfloat16
I32 = jnp.int32
NT = (((1,), (1,)), ((), ()))
NN = (((1,), (0,)), ((), ()))


def halves(x):
    high = x.astype(BF16)
    return high, (x - high.astype(F32)).astype(BF16)


def dot(a, b, dims=NN):
    return lax.dot_general(a, b, dims, preferred_element_type=F32)


OWNED = (0, 1, 4, 3, 8, 9, 11, 12, 2, 5, 7, 6, 13, 10, 15, 14)


def select(hot, x):
    wide = x.shape[1]
    y = dot(hot, jnp.concatenate(halves(x), axis=1))
    return y[:, :wide] + y[:, wide:]


PIECE = 4


def kernel(slots, queries, user_blocks, item_blocks, width, *refs):
    inputs, out, local = refs[:7], refs[7], refs[8:15]
    (
        vhi, vlo, hits, msg1, recv1, xsend, xrecv, msg2, recv2, msg3, recv3,
        meta_r_out, meta_r, meta_c_out, meta_c, pick_r, pick_rt, pick_c,
        load_sem, vals_sem, back_sem, sem,
    ) = refs[15:]
    hist, ideg, udeg, vals, rows, cols, count = local
    n = queries
    span = slots * n
    items = lax.axis_index("items")
    user = lax.axis_index("users")
    z, y_hi, core = items // 4, lax.rem(items // 2, 2), lax.rem(items, 2)
    depth, run = n // 2, n // 4
    partner = {"items": items + 1 - 2 * core}

    def chip_of(z, y):
        return ((z // run) * 2 + y) * run + lax.rem(z, run)

    chip = chip_of(z, y_hi)

    owned = OWNED if n == len(OWNED) else tuple(range(n))

    away = [(dz, dy) for dz in range(depth) for dy in range(2) if dz or dy]
    away.sort(key=lambda d: -min(d[0], depth - d[0]) - 10 * d[1])

    def chips(action):
        for dz, dy in away:
            there, y = lax.rem(z + dz, depth), lax.rem(y_hi + dy, 2)
            action(chip_of(there, y), {"items": (there * 2 + y) * 2 + core})

    def users(action):
        @pl.loop(1, n)
        def _(i):
            action(lax.rem(user + i, n))

    def send(src, dst, send_k, recv_sem, where):
        pltpu.make_async_remote_copy(
            src, dst, sem.at[send_k], recv_sem, device_id=where, device_id_type=MESH
        ).start()

    def part(ref, i, size=slots):
        return ref.at[pl.ds(pl.multiple_of(i * size, 8), size)]

    def wait(ref, count_rows, k):
        piece = ref.at[pl.ds(0, count_rows)]
        pltpu.make_async_copy(piece, piece, sem.at[k]).wait()

    barrier = pltpu.get_barrier_semaphore()
    loads = {i: pltpu.make_async_copy(inputs[i], local[i], load_sem.at[i]) for i in (0, 1, 2, 4, 5, 6)}
    pieces = []
    for i in range(0, slots, PIECE):
        here = pl.ds(i, PIECE)
        pieces.append(pltpu.make_async_copy(inputs[3].at[here], vals.at[here], vals_sem.at[i // PIECE]))
    for load in (loads[4], loads[5], loads[6], loads[0], loads[1], *pieces, loads[2]):
        load.start()

    def greet(where):
        pl.semaphore_signal(barrier, inc=1, device_id=where, device_id_type=MESH)

    chips(lambda c, where: greet(where))
    users(lambda p: greet({"users": p}))
    greet(partner)

    lane = lax.broadcasted_iota(I32, (1, width), 1)
    sub = lax.broadcasted_iota(I32, (slots, width), 0)
    for i in (4, 5, 6):
        loads[i].wait()
    mrow = jnp.zeros((1, width), I32)
    mcol = jnp.zeros((1, width), I32)
    colv = jnp.zeros((slots, width), I32)
    alive = count[0, 0]
    for t in range(slots):
        r, c = rows[0, 0, t], cols[0, 0, t]
        live = t < alive
        mrow = jnp.where(lane == lax.rem(chip * slots + t, width), jnp.where(live, r, -1), mrow)
        mcol = jnp.where(lane == lax.rem(user * slots + t, width), jnp.where(live, c, -1), mcol)
        colv = jnp.where(sub == t, c, colv)
    meta_r_out[...] = mrow
    meta_c_out[...] = mcol
    meta_r[chip] = mrow
    meta_c[user] = mcol

    loads[0].wait()
    hlen = hist.shape[1]
    bits = width.bit_length() - 1
    colw = jnp.concatenate([colv] * (hlen // width), axis=1) + items * item_blocks
    lane_id = lax.broadcasted_iota(I32, (width, hlen), 0)
    for q in range(n):
        h = hist[q : q + 1, :]
        block = lax.shift_right_logical(h, bits) == colw
        spot = (h & (width - 1)) == lane_id
        hits[pl.ds(owned.index(q), slots, stride=n), :] = dot(
            jnp.where(block, 1.0, 0.0).astype(BF16), jnp.where(spot, 1.0, 0.0).astype(BF16), NT
        )

    loads[1].wait()

    for t in range(slots):
        if t % PIECE == 0:
            pieces[t // PIECE].wait()
        degree = ideg[pl.ds(cols[0, 0, t], 1), :]
        high, low = halves(vals[t] * lax.rsqrt(degree.astype(F32)))
        vhi[t] = high
        vlo[t] = low
        h = hits[pl.ds(t * n, n), :].astype(BF16)
        msg1[pl.ds(t, n, stride=slots), :] = dot(h, high, NT) + dot(h, low, NT)

    pl.semaphore_wait(barrier, 2 * (n - 1) + 1)

    def forth(c, where):
        send(meta_r_out, meta_r.at[chip], 1, sem.at[2], where)
        send(part(msg1, c), part(recv1, chip), 5, sem.at[6], where)

    chips(forth)
    part(recv1, chip)[...] = part(msg1, chip)[...]

    def gathered(ref, k):
        ids = jnp.zeros((1, width), I32)
        for i in range(k * width // slots, min(n, -(-(k + 1) * width // slots))):
            from_i = (lane >= i * slots - k * width) & (lane < (i + 1) * slots - k * width)
            ids = jnp.where(from_i, ref[i], ids)
        return ids

    wait(meta_r, n - 1, 2)
    block = lax.broadcasted_iota(I32, (width, width), 0)
    for k in range(span // width):
        at = slice(k * width, (k + 1) * width)
        pick_r[:, at] = jnp.where(gathered(meta_r, k) == block[:user_blocks], 1.0, 0.0).astype(BF16)

    wait(recv1, slots * (n - 1), 6)
    acc = select(pick_r[...], recv1[...])
    xsend[...] = acc
    cross = pltpu.make_async_remote_copy(
        xsend, xrecv, sem.at[7], sem.at[8], device_id=partner, device_id_type=MESH
    )
    cross.start()
    for k in range(span // width):
        hot = jnp.where(gathered(meta_r, k) == block, 1.0, 0.0)
        pick_rt[k * width : (k + 1) * width, :] = hot.T.astype(BF16)
    loads[2].wait()
    cross.wait()
    weights = (acc + xrecv[...]) / udeg[...].astype(F32)
    msg2[...] = select(pick_rt[:, :user_blocks], weights)
    mine = back_sem.at[chip // run]
    chips(lambda c, where: send(part(msg2, c), part(recv2, chip), 9, mine, where))
    part(recv2, chip)[...] = part(msg2, chip)[...]

    users(lambda p: send(meta_c_out, meta_c.at[user], 3, sem.at[4], {"users": p}))

    @pl.loop(0, 4)
    def _(j):
        g = lax.rem(z // run + lax.rem(j, 2), 2) * 2 + lax.rem(y_hi + j // 2, 2)
        for came, senders in ((j == 0, run - 1), (j > 0, run)):

            @pl.when(came)
            def _():
                piece = recv2.at[pl.ds(0, slots * senders)]
                pltpu.make_async_copy(piece, piece, back_sem.at[g]).wait()

        for t in range(slots):
            spots = pl.ds(g * (run * slots) + t, run, stride=slots)
            x = recv2[spots, :]
            high = x.astype(BF16).astype(F32)
            x = jnp.concatenate([high, x - high], axis=0).astype(BF16)
            y = dot(x, vhi[t]) + dot(x, vlo[t])
            msg3[spots, :] = y[:run] + y[run:]

        for m in range(run):
            c, u = g * run + m, owned[m]
            for k in range(1, 4):
                u = jnp.where(g == k, owned[k * run + m], u)

            @pl.when(u != user)
            def _():
                send(part(msg3, c), part(recv3, user), 11, sem.at[12], {"users": u})

    own = 0
    for c in range(1, n):
        own = jnp.where(user == owned[c], c, own)
    part(recv3, user)[...] = part(msg3, own)[...]
    wait(meta_c, n - 1, 4)
    block = lax.broadcasted_iota(I32, (item_blocks, width), 0)
    for k in range(span // width):
        at = slice(k * width, (k + 1) * width)
        pick_c[:, at] = jnp.where(gathered(meta_c, k) == block, 1.0, 0.0).astype(BF16)
    wait(recv3, slots * (n - 1), 12)
    out[...] = select(pick_c[...], recv3[...])

    wait(meta_r, n - 1, 1)
    wait(meta_c, n - 1, 3)
    wait(msg1, slots * (n - 1), 5)
    wait(msg2, slots * (n - 1), 9)
    wait(msg3, slots * (n - 1), 11)


def body(histories, item_degree, user_degree, tile_values, tile_rows, tile_cols, tile_count):
    queries = histories.shape[0]
    slots, width = tile_values.shape[2], tile_values.shape[-1]
    item_blocks = item_degree.shape[0] // width
    user_blocks = user_degree.shape[0] // width
    span = slots * queries
    vmem = pl.BlockSpec(memory_space=pltpu.VMEM)
    panel = pltpu.VMEM((span, width), F32)
    scores = pl.pallas_call(
        functools.partial(kernel, slots, queries, user_blocks, item_blocks, width),
        out_shape=jax.ShapeDtypeStruct((item_blocks, width), F32),
        in_specs=[pl.BlockSpec(memory_space=pltpu.HBM)] * 7,
        out_specs=vmem,
        scratch_shapes=[
            pltpu.VMEM(histories.shape, I32),
            pltpu.VMEM((item_blocks, width), I32),
            pltpu.VMEM((user_blocks, width), I32),
            pltpu.VMEM((slots, width, width), F32),
            pltpu.SMEM(tile_rows.shape, I32),
            pltpu.SMEM(tile_cols.shape, I32),
            pltpu.SMEM(tile_count.shape, I32),
            pltpu.VMEM((slots, width, width), BF16),
            pltpu.VMEM((slots, width, width), BF16),
            panel, panel, panel,
            pltpu.VMEM((user_blocks, width), F32),
            pltpu.VMEM((user_blocks, width), F32),
            panel, panel, panel, panel,
            pltpu.VMEM((1, width), I32),
            pltpu.VMEM((queries, 1, width), I32),
            pltpu.VMEM((1, width), I32),
            pltpu.VMEM((queries, 1, width), I32),
            pltpu.VMEM((user_blocks, span), BF16),
            pltpu.VMEM((span, width), BF16),
            pltpu.VMEM((item_blocks, span), BF16),
            pltpu.SemaphoreType.DMA((7,)),
            pltpu.SemaphoreType.DMA((slots // PIECE,)),
            pltpu.SemaphoreType.DMA((4,)),
            pltpu.SemaphoreType.DMA((13,)),
        ],
        compiler_params=pltpu.CompilerParams(
            collective_id=0, has_side_effects=True, vmem_limit_bytes=32 * 1024 * 1024
        ),
        cost_estimate=pl.CostEstimate(flops=10**8, bytes_accessed=4 * 10**6, transcendentals=0),
    )(*[pltpu.with_memory_space_constraint(x, pltpu.HBM) for x in (
        histories,
        item_degree.reshape(item_blocks, width),
        user_degree.reshape(user_blocks, width),
        tile_values.reshape(slots, width, width),
        tile_rows, tile_cols,
    )], tile_count)
    return scores.reshape(1, item_blocks * width)


def solution(mesh):
    in_specs = (
        P(),
        P("items"),
        P("users"),
        P("users", "items", None, None, None),
        P("users", "items", None),
        P("users", "items", None),
        P("users", "items"),
    )
    out_specs = P("users", "items")
    return jax.shard_map(body, mesh=mesh, in_specs=in_specs, out_specs=out_specs, check_vma=False)
```
